1024 devices in a mesh: samp: 16 (over x, z_lo), feat: 64 (over z_hi, y, core).
Axes of the slice: x: 4, y: 8, z: 16 (z_hi: 4, z_lo: 4; z = z_hi * 4 + z_lo), core: 2. Of those that a mesh axis runs over, the one named last changes fastest.
Arguments:
- data: float32 [16384, 16384], P('samp', 'feat'), may hold values from -0.1118034 to 0.1118034, as said below
- targets: float32 [16384, 128], P(('samp', 'feat')), may hold values from -36 to 36
- coef: float32 [16384, 128], P('feat'), may hold values from -6 to 6
- coef_dual: float32 [16384, 128], P('feat'), may hold values from -3 to 3
- tile_coef_dual: float32 [16, 16384, 128], P('samp', 'feat'), may hold values from -3 to 3
- share: float32 [16384, 128], P(('samp', 'feat')), may hold values from -36 to 36
- share_dual: float32 [16384, 128], P('samp'), may hold values from -6 to 6
- tile_share: float32 [64, 16384, 128], P('feat', 'samp'), may hold values from -6 to 6
Outputs:
- coef_out: float32 [16384, 128], P('feat')
- coef_dual_out: float32 [16384, 128], P('feat')
- tile_coef_dual_out: float32 [16, 16384, 128], P('samp', 'feat')
- share_out: float32 [16384, 128], P(('samp', 'feat'))
- share_dual_out: float32 [16384, 128], P('samp')
- tile_share_out: float32 [64, 16384, 128], P('feat', 'samp')
The draws below stay inside these ranges and needn't reach their ends.
Inputs may be any that keep to these rules, and one draw needn't show every extreme that they name: `data`: independent entries of mean zero and variance 1 / 1280.
All inputs are finite; a program needn't handle non-finite values.
Results may differ from the reference program's by a relative error of at most 0.0001.
Values sent between devices are 32-bit elements; how exact they have to be, the bound alone decides.
A program may use at most 32 MiB of HBM per device.

```python
import jax
import jax.numpy as jnp
from jax import lax

K = 128
FEATURES = 16384
S_DEV = 1024
ITERS = 2
CHEB = 5
F_DEV = 256
SAMPLES = 16384
N_SAMP = 16
N_FEAT = 64


def draw_data(key, part):
    scale = 1.0 / jnp.sqrt(jnp.float32(S_DEV + F_DEV))
    values = jnp.clip(jax.random.normal(key, (SAMPLES, FEATURES), jnp.float32), -4.0, 4.0)
    return values * scale


def block_levels(rng, extent, pieces, smallest, top_value):
    gain, own = 1.0, jax.random.fold_in(rng, 6)
    for dim, blocks in pieces:
        steps = jnp.exp(jax.random.uniform(jax.random.fold_in(own, dim), (blocks,), jnp.float32, smallest / len(pieces), top_value / len(pieces)))
        gain = gain * jnp.repeat(steps, extent[dim] // blocks).reshape([-1 if axis == dim else 1 for axis in range(len(extent))])
    return gain


def normal_values(stream_key, extent, spread, reach, cuts=(), kind=jnp.bfloat16):
    array = jax.random.normal(stream_key, extent, jnp.float32) * spread
    if len(cuts) > 0:
        array = block_levels(stream_key, extent, cuts, -0.22, 0.18) * array
    return jnp.clip(array, min=-reach, max=reach).astype(kind)


def setup_inputs(seed: int = 0) -> dict:
    streams_of = jax.random.split(jax.random.key(seed), 9)
    return {
        "data": draw_data(jax.random.fold_in(streams_of[8], 71), 0),
        "targets": normal_values(streams_of[1], (SAMPLES, K), 6.0, 36.0, ((0, 1024),), jnp.float32),
        "coef": normal_values(streams_of[2], (FEATURES, K), 1.0, 6.0, ((0, 64),), jnp.float32),
        "coef_dual": normal_values(streams_of[3], (FEATURES, K), 0.5, 3.0, ((0, 64),), jnp.float32),
        "tile_coef_dual": normal_values(streams_of[4], (N_SAMP, FEATURES, K), 0.5, 3.0, ((0, 16), (1, 64)), jnp.float32),
        "share": normal_values(streams_of[5], (SAMPLES, K), 6.0, 36.0, ((0, 1024),), jnp.float32),
        "share_dual": normal_values(streams_of[6], (SAMPLES, K), 1.0, 6.0, ((0, 16),), jnp.float32),
        "tile_share": normal_values(streams_of[7], (N_FEAT, SAMPLES, K), 1.0, 6.0, ((0, 64), (1, 16)), jnp.float32),
    }


cheb_low = 1.0
cheb_high = 3.2
l1_weight = 0.2
huber_width = 4.0


def chebyshev(apply_fn, rhs, start):
    theta = (cheb_high + cheb_low) / 2.0
    delta = (cheb_high - cheb_low) / 2.0
    sigma = theta / delta
    iterate = start
    resid = rhs - apply_fn(iterate)
    search = resid / theta
    rho_old = 1.0 / sigma
    for step in range(CHEB):
        iterate = iterate + search
        if step + 1 < CHEB:
            resid = resid - apply_fn(search)
            rho_new = 1.0 / (2.0 * sigma - rho_old)
            search = rho_new * rho_old * search + (2.0 * rho_new / delta) * resid
            rho_old = rho_new
    return iterate


def reference(data, targets, coef, coef_dual, tile_coef_dual, share, share_dual, tile_share):
    high = lax.Precision.HIGHEST
    blocks = data.reshape(N_SAMP, S_DEV, N_FEAT, F_DEV)
    for sweep in range(ITERS):
        value = coef - coef_dual
        half_coef = value - jnp.clip(value, -l1_weight, l1_weight)
        resid_t = share - share_dual - targets
        half_share = targets + resid_t - jnp.clip(resid_t / 2.0, -huber_width, huber_width)
        shares_grouped = jnp.transpose(tile_share.reshape(N_FEAT, N_SAMP, S_DEV, K), (1, 0, 2, 3))
        duals_grouped = share_dual.reshape(N_SAMP, S_DEV, K)
        coef_now = coef

        def group(items):
            tiles, xt_group, ys_group, dual_group = items
            tiles = jnp.transpose(tiles, (1, 0, 2))
            start = coef_now.reshape(N_FEAT, F_DEV, K) - xt_group.reshape(N_FEAT, F_DEV, K)
            outs_in = ys_group + dual_group[None]

            def apply_fn(vector):
                inner = jnp.einsum("jsf,jfk->jsk", tiles, vector, precision=high)
                return vector + jnp.einsum("jsf,jsk->jfk", tiles, inner, precision=high)

            rhs = start + jnp.einsum("jsf,jsk->jfk", tiles, outs_in, precision=high)
            proj_x = chebyshev(apply_fn, rhs, start)
            proj_y = jnp.einsum("jsf,jfk->jsk", tiles, proj_x, precision=high)
            return proj_x, proj_y

        proj_coef, proj_share = lax.map(group, (blocks, tile_coef_dual, shares_grouped, duals_grouped))
        coef_new = (half_coef + jnp.sum(proj_coef, axis=0).reshape(FEATURES, K)) / (N_SAMP + 1)
        share_sum = jnp.sum(proj_share, axis=1).reshape(SAMPLES, K)
        excess = (half_share - share_sum) / (N_FEAT + 1)
        share = half_share - excess
        tile_share = jnp.transpose(proj_share, (1, 0, 2, 3)).reshape(N_FEAT, SAMPLES, K) + excess[None]
        share_dual = share_dual + excess
        coef_dual = coef_dual + half_coef - coef_new
        tile_coef_dual = tile_coef_dual + proj_coef.reshape(N_SAMP, FEATURES, K) - coef_new[None]
        coef = coef_new
    return (coef, coef_dual, tile_coef_dual, share, share_dual, tile_share)
```

```python
import functools

import jax
import jax.numpy as jnp
from jax import lax
from jax.experimental import pallas as pl
from jax.experimental.pallas import tpu as pltpu
from jax.sharding import PartitionSpec as P

ITERS = 2
CHEB = 5

cheb_low = 1.0
cheb_high = 3.2
l1_weight = 0.2
huber_width = 4.0

NX, NL, NH, NY, NC = 4, 4, 4, 8, 2
B = 16
K = 128

MESH = pl.DeviceIdType.MESH
f32 = jnp.float32
bf16 = jnp.bfloat16


def split(v):
    hi = v.astype(bf16)
    return hi, (v - hi.astype(f32)).astype(bf16)


def mul(lhs_hi, lhs_lo, v):
    hi, lo = split(v)
    both = jnp.dot(lhs_hi, jnp.concatenate([hi, lo], axis=1), preferred_element_type=f32)
    return both[:, :K] + both[:, K:] + jnp.dot(lhs_lo, hi, preferred_element_type=f32)


def far_first(n):
    return sorted(range(1, n), key=lambda p: -min(p, n - p))


def body(
    data, targets, coef, cdual, tdual, share, sdual, tshare,
    o_coef, o_cdual, o_tdual, o_share, o_sdual, o_tshare,
    a32, a_hi, a_lo, at_hi, at_lo, gram_hi, gram_lo,
    v_targets, v_coef, v_cdual, v_tdual, v_share, v_sdual, v_tshare,
    ps, pair_in, y_out, y_in, h_out, h_in, exc, zc, x_in, l_out, l_in, cnew,
    load_sem, store_sem, send_sem, recv_sem,
):
    half = NY * NH * B
    rows = NC * half
    feats = NX * NL * B
    s, f = lax.axis_index("samp"), lax.axis_index("feat")
    x, l = s // NL, s % NL
    h, y, c = f // (NY * NC), (f // NC) % NY, f % NC
    other = 1 - c

    def feat_dev(h_, y_, c_):
        return (s, (h_ * NY + y_) * NC + c_)

    def samp_dev(x_, l_):
        return (x_ * NL + l_, f)

    y_order, h_order, x_order, l_order = far_first(NY), far_first(NH), far_first(NX), far_first(NL)

    loads = []

    def load(src, dst):
        copy = pltpu.make_async_copy(src, dst, load_sem.at[len(loads)])
        copy.start()
        loads.append(copy)
        return copy

    data_loads = [load(data.at[k, :, m], a32.at[m, :, k]) for m in range(NC) for k in range(NH)]
    out_loads = [
        load(src.at[k, :, m], dst.at[m, :, k])
        for src, dst in ((tshare, v_tshare), (sdual, v_sdual))
        for m in range(NC)
        for k in range(NH)
    ]
    small_loads = [
        load(coef, v_coef.at[0]),
        load(tdual, v_tdual.at[0]),
        load(cdual, v_cdual.at[0]),
        load(targets, v_targets),
        load(share, v_share),
    ]

    barrier = pltpu.get_barrier_semaphore()
    partners = (
        [feat_dev(h, y, other)]
        + [feat_dev(h, (y + p) % NY, c) for p in range(1, NY)]
        + [feat_dev((h + p) % NH, y, c) for p in range(1, NH)]
        + [samp_dev((x + p) % NX, l) for p in range(1, NX)]
        + [samp_dev(x, (l + p) % NL) for p in range(1, NL)]
    )
    for who in partners:
        pl.semaphore_signal(barrier, inc=1, device_id=who, device_id_type=MESH)

    for copy in data_loads:
        copy.wait()
    a = a32[...].reshape(rows, feats)
    hi, lo = split(a)
    a_hi[...] = hi.reshape(NC, half, feats)
    a_lo[...] = lo.reshape(NC, half, feats)
    hi, lo = split(a.T)
    at_hi[...] = hi
    at_lo[...] = lo
    gram = jnp.zeros((feats, feats), f32)
    for m in range(NC):
        cols = slice(m * half, (m + 1) * half)
        both = jnp.dot(
            at_hi[:, cols], jnp.concatenate([a_hi[m], a_lo[m]], axis=1), preferred_element_type=f32
        )
        gram += both[:, :feats] + both[:, feats:]
        gram += jnp.dot(at_lo[:, cols], a_hi[m], preferred_element_type=f32)
    hi, lo = split(gram)
    gram_hi[...] = hi
    gram_lo[...] = lo

    for copy in out_loads + small_loads:
        copy.wait()

    def gram_mul(v):
        return mul(gram_hi[...], gram_lo[...], v)

    sent = []
    count = [0]

    def remote(src, dst, who):
        k = count[0]
        count[0] += 1
        copy = pltpu.make_async_remote_copy(
            src_ref=src, dst_ref=dst, send_sem=send_sem.at[k], recv_sem=recv_sem.at[k],
            device_id=who, device_id_type=MESH,
        )
        copy.start()
        sent.append(copy)
        return copy

    stores = []

    def store(src, dst):
        copy = pltpu.make_async_copy(src, dst, store_sem.at[len(stores)])
        copy.start()
        stores.append(copy)

    theta = (cheb_high + cheb_low) / 2.0
    delta = (cheb_high - cheb_low) / 2.0
    sigma = theta / delta

    for it in range(ITERS):
        last = it + 1 == ITERS
        start = v_coef[it] - v_tdual[it]
        outs = (v_tshare[...] + v_sdual[...]).reshape(rows, K)

        resid = mul(at_hi[...], at_lo[...], outs) - gram_mul(start)
        search = resid * (1.0 / theta)
        z = start + search
        rho_old = 1.0 / sigma
        for step in range(CHEB - 1):
            resid = resid - search - gram_mul(search)
            rho_new = 1.0 / (2.0 * sigma - rho_old)
            search = (rho_new * rho_old) * search + (2.0 * rho_new / delta) * resid
            rho_old = rho_new
            z = z + search
        zc[it] = z.reshape(NX, NL, B, K)
        if it == 0:
            pl.semaphore_wait(barrier, len(partners))

        to_x = [
            remote(zc.at[it, (x + p) % NX], x_in.at[it, p - 1], samp_dev((x + p) % NX, l))
            for p in x_order
        ]

        z_hi, z_lo = split(z)
        z_both = jnp.concatenate([z_hi, z_lo], axis=1)

        def forward(m):
            both = jnp.dot(a_hi[m], z_both, preferred_element_type=f32)
            got = both[:, :K] + both[:, K:] + jnp.dot(a_lo[m], z_hi, preferred_element_type=f32)
            ps[it, m] = got.reshape(NY, NH, B, K)

        forward(other)
        to_pair = {
            p: remote(
                ps.at[it, other, (y + p) % NY], pair_in.at[it, (y + p) % NY], feat_dev(h, y, other)
            )
            for p in y_order + [0]
        }
        forward(c)

        to_y = {}
        for p in y_order:
            to_pair[p].wait_recv()
            q = (y + p) % NY
            y_out[it, p] = ps[it, c, q] + pair_in[it, q]
            to_y[p] = remote(y_out.at[it, p], y_in.at[it, p - 1], feat_dev(h, q, c))
        to_pair[0].wait_recv()
        own = ps[it, c, y] + pair_in[it, y]

        for copy in to_x:
            copy.wait_recv()
        l_out[it] = zc[it, x] + x_in[it, 0] + x_in[it, 1] + x_in[it, 2] if NX == 4 else sum(
            [x_in[it, k] for k in range(NX - 1)], zc[it, x]
        )
        to_l = [
            remote(l_out.at[it, (l + p) % NL], l_in.at[it, p - 1], samp_dev(x, (l + p) % NL))
            for p in l_order
        ]

        for p in y_order:
            to_y[p].wait_recv()
            own = own + y_in[it, p - 1]
        h_out[it] = own
        to_h = [
            remote(h_out.at[it, (h + p) % NH], h_in.at[it, p - 1], feat_dev((h + p) % NH, y, c))
            for p in h_order
        ]

        value = v_coef[it] - v_cdual[it]
        half_coef = value - jnp.clip(value, -l1_weight, l1_weight)
        zc[it + ITERS] = half_coef.reshape(NX, NL, B, K)
        for copy in to_l:
            copy.wait_recv()
        mine = zc[it + ITERS, x, l] + l_out[it, l]
        for k in range(NL - 1):
            mine = mine + l_in[it, k]
        cnew[it, x, l] = mine * (1.0 / (NX * NL + 1))
        from_l = [
            remote(cnew.at[it, x, l], cnew.at[it, x, l], samp_dev(x, (l + p) % NL)) for p in l_order
        ]

        resid_t = v_share[...] - v_sdual[c, y, h] - v_targets[...]
        half_share = v_targets[...] + resid_t - jnp.clip(resid_t * 0.5, -huber_width, huber_width)
        for copy in to_h:
            copy.wait_recv()
        total = h_out[it, h]
        for k in range(NH - 1):
            total = total + h_in[it, k]
        own_excess = (half_share - total) * (1.0 / (NH * NY * NC + 1))
        exc[it, c, y, h] = own_excess
        v_share[...] = half_share - own_excess
        from_h = [
            remote(exc.at[it, c, y, h], exc.at[it, c, y, h], feat_dev((h + p) % NH, y, c))
            for p in h_order
        ]

        for copy in from_l:
            copy.wait_recv()
        from_x = [
            remote(cnew.at[it, x], cnew.at[it, x], samp_dev((x + p) % NX, l)) for p in x_order
        ]

        for copy in from_h:
            copy.wait_recv()
        from_y = {
            p: remote(exc.at[it, c, y], exc.at[it, c, y], feat_dev(h, (y + p) % NY, c))
            for p in y_order
        }
        from_pair = [remote(exc.at[it, c, y], exc.at[it, c, y], feat_dev(h, y, other))]

        for copy in from_x:
            copy.wait_recv()
        coef_new = cnew[it].reshape(feats, K)
        v_coef[it + 1] = coef_new
        v_cdual[it + 1] = v_cdual[it] + half_coef - coef_new
        v_tdual[it + 1] = v_tdual[it] + zc[it].reshape(feats, K) - coef_new
        if last:
            store(v_coef.at[it + 1], o_coef)
            store(v_cdual.at[it + 1], o_cdual)
            store(v_tdual.at[it + 1], o_tdual)
            store(v_share, o_share)

        for p in reversed(y_order):
            from_y[p].wait_recv()
            q = (y - p + NY) % NY
            from_pair.append(
                remote(exc.at[it, c, q], exc.at[it, c, q], feat_dev(h, y, other))
            )
        for copy in from_pair:
            copy.wait_recv()
        v_sdual[...] = v_sdual[...] + exc[it]
        v_tshare[...] = ps[it] + exc[it]
        if last:
            for src, dst in ((v_sdual, o_sdual), (v_tshare, o_tshare)):
                for m in range(NC):
                    for k in range(NH):
                        store(src.at[m, :, k], dst.at[k, :, m])

    for copy in sent:
        copy.wait_send()
    for copy in stores:
        copy.wait()


def shards(data, targets, coef, cdual, tdual, share, sdual, tshare):
    feats = NX * NL * B
    whole = (NH, NY, NC, B)
    perm = (NC, NY, NH, B)
    half = NY * NH * B
    hbm = pl.BlockSpec(memory_space=pltpu.HBM)
    copies = ITERS * (2 * NC * (NY - 1) + 2 * (NH + NX + NL - 3) + (NC - 1) * 2 * NY - (NC - 1) * 0)
    vm = pltpu.VMEM
    outs = pl.pallas_call(
        body,
        out_shape=[
            jax.ShapeDtypeStruct((feats, K), f32),
            jax.ShapeDtypeStruct((feats, K), f32),
            jax.ShapeDtypeStruct((feats, K), f32),
            jax.ShapeDtypeStruct((B, K), f32),
            jax.ShapeDtypeStruct(whole + (K,), f32),
            jax.ShapeDtypeStruct(whole + (K,), f32),
        ],
        in_specs=[hbm] * 8,
        out_specs=[hbm] * 6,
        scratch_shapes=[
            vm(perm + (feats,), f32),
            vm((NC, half, feats), bf16),
            vm((NC, half, feats), bf16),
            vm((feats, NC * half), bf16),
            vm((feats, NC * half), bf16),
            vm((feats, feats), bf16),
            vm((feats, feats), bf16),
            vm((B, K), f32),
            vm((ITERS + 1, feats, K), f32),
            vm((ITERS + 1, feats, K), f32),
            vm((ITERS + 1, feats, K), f32),
            vm((B, K), f32),
            vm(perm + (K,), f32),
            vm(perm + (K,), f32),
            vm((ITERS,) + perm + (K,), f32),
            vm((ITERS, NY, NH, B, K), f32),
            vm((ITERS, NY, NH, B, K), f32),
            vm((ITERS, NY - 1, NH, B, K), f32),
            vm((ITERS, NH, B, K), f32),
            vm((ITERS, NH - 1, B, K), f32),
            vm((ITERS,) + perm + (K,), f32),
            vm((2 * ITERS, NX, NL, B, K), f32),
            vm((ITERS, NX - 1, NL, B, K), f32),
            vm((ITERS, NL, B, K), f32),
            vm((ITERS, NL - 1, B, K), f32),
            vm((ITERS, NX, NL, B, K), f32),
            pltpu.SemaphoreType.DMA((3 * NC * NH + 5,)),
            pltpu.SemaphoreType.DMA((2 * NC * NH + 4,)),
            pltpu.SemaphoreType.DMA((copies,)),
            pltpu.SemaphoreType.DMA((copies,)),
        ],
        compiler_params=pltpu.CompilerParams(
            collective_id=0, has_side_effects=True, vmem_limit_bytes=48 * 1024 * 1024
        ),
    )(
        data.reshape(whole + (feats,)), targets, coef, cdual, tdual[0], share,
        sdual.reshape(whole + (K,)), tshare.reshape(whole + (K,)),
    )
    coef, cdual, tdual, share, sdual, tshare = outs
    rows = NC * half
    return (coef, cdual, tdual[None], share, sdual.reshape(rows, K), tshare.reshape(1, rows, K))


def solution(mesh):
    return jax.shard_map(
        shards,
        mesh=mesh,
        in_specs=(
            P("samp", "feat"),
            P(("samp", "feat"), None),
            P("feat", None),
            P("feat", None),
            P("samp", "feat", None),
            P(("samp", "feat"), None),
            P("samp", None),
            P("feat", "samp", None),
        ),
        out_specs=(
            P("feat", None),
            P("feat", None),
            P("samp", "feat", None),
            P(("samp", "feat"), None),
            P("samp", None),
            P("feat", "samp", None),
        ),
        check_vma=False,
    )
```

```python
import functools

import jax
import jax.numpy as jnp
from jax import lax
from jax.experimental import pallas as pl
from jax.experimental.pallas import tpu as pltpu
from jax.sharding import PartitionSpec as P

ITERS = 2
CHEB = 5

cheb_low = 1.0
cheb_high = 3.2
l1_weight = 0.2
huber_width = 4.0

NX, NL, NH, NY, NC = 4, 4, 4, 8, 2
B = 16
K = 128
NG = 2
VMEM_MIB = 60

MESH = pl.DeviceIdType.MESH
f32 = jnp.float32
bf16 = jnp.bfloat16


def split(v):
    hi = v.astype(bf16)
    return hi, (v - hi.astype(f32)).astype(bf16)


def mul2(lhs_hi, lhs_lo, hi, lo):
    n = hi.shape[1]
    both = jnp.dot(lhs_hi, jnp.concatenate([hi, lo], axis=1), preferred_element_type=f32)
    return both[:, :n] + both[:, n:] + jnp.dot(lhs_lo, hi, preferred_element_type=f32)


def mul(lhs_hi, lhs_lo, v):
    return mul2(lhs_hi, lhs_lo, *split(v))


def far_first(n):
    return sorted(range(1, n), key=lambda p: -min(p, n - p))


def body(
    data, targets, coef, cdual, tdual, share, sdual, tshare,
    o_coef, o_cdual, o_tdual, o_share, o_sdual, o_tshare,
    a32, a_hi, a_lo, at_hi, at_lo, w_hi, w_lo, gram_hi, gram_lo, q_hi, q_lo,
    v_st, v_coef, v_cdual, v_tdual, v_sdual, v_tshare,
    ps, pair_in, y_out, y_in, h_all, exc, zc, half_c, x_in, l_all, cnew,
    load_sem, send_sem, recv_sem,
):
    half = NY * NH * B
    rows = NC * half
    feats = NX * NL * B
    s, f = lax.axis_index("samp"), lax.axis_index("feat")
    x, l = s // NL, s % NL
    h, y, c = f // (NY * NC), (f // NC) % NY, f % NC
    other = 1 - c

    def feat_dev(h_, y_, c_):
        return (s, (h_ * NY + y_) * NC + c_)

    def samp_dev(x_, l_):
        return (x_ * NL + l_, f)

    y_order, h_order, x_order, l_order = far_first(NY), far_first(NH), far_first(NX), far_first(NL)
    groups = [slice(g * (NH // NG), (g + 1) * (NH // NG)) for g in range(NG)]

    barrier = pltpu.get_barrier_semaphore()
    partners = (
        [feat_dev((h + p) % NH, y, c) for p in h_order]
        + [feat_dev(h, (y + p) % NY, c) for p in y_order]
        + [samp_dev((x + p) % NX, l) for p in x_order]
        + [samp_dev(x, (l + p) % NL) for p in l_order]
        + [feat_dev(h, y, other)]
    )
    for who in partners:
        pl.semaphore_signal(barrier, inc=1, device_id=who, device_id_type=MESH)

    loads = []

    def load(src, dst):
        copy = pltpu.make_async_copy(src, dst, load_sem.at[len(loads)])
        copy.start()
        loads.append(copy)
        return copy

    data_loads = [load(data.at[k, :, m], a32.at[m, :, k]) for m in range(NC) for k in range(NH)]
    out_loads = [
        load(src.at[k, :, m], dst.at[m, :, k])
        for src, dst in ((tshare, v_tshare), (sdual, v_sdual))
        for m in range(NC)
        for k in range(NH)
    ]
    small_loads = [
        load(coef, v_coef.at[0]),
        load(tdual, v_tdual.at[0]),
        load(cdual, v_cdual.at[0]),
        load(share, v_st.at[0, h]),
        load(targets, v_st.at[1, h]),
    ]

    for copy in data_loads:
        copy.wait()
    gram = jnp.zeros((feats, feats), f32)
    for m in range(NC):
        a = a32[m].reshape(half, feats)
        hi, lo = split(a)
        a_hi[m] = hi
        a_lo[m] = lo
        t_hi, t_lo = split(a.T)
        at_hi[m] = t_hi
        at_lo[m] = t_lo
        gram += mul2(t_hi, t_lo, hi, lo)
    hi, lo = split(gram)
    gram_hi[...] = hi
    gram_lo[...] = lo

    for copy in out_loads + small_loads:
        copy.wait()

    def gram_mul(v):
        return mul(gram_hi[...], gram_lo[...], v)

    sent = []
    count = [0]

    def remote(src, dst, who):
        k = count[0]
        count[0] += 1
        copy = pltpu.make_async_remote_copy(
            src_ref=src, dst_ref=dst, send_sem=send_sem.at[k], recv_sem=recv_sem.at[k],
            device_id=who, device_id_type=MESH,
        )
        copy.start()
        sent.append(copy)
        return copy

    theta = (cheb_high + cheb_low) / 2.0
    delta = (cheb_high - cheb_low) / 2.0
    sigma = theta / delta

    def chebyshev(resid):
        search = resid * (1.0 / theta)
        z = search
        rho_old = 1.0 / sigma
        for step in range(CHEB - 1):
            resid = resid - search - gram_mul(search)
            rho_new = 1.0 / (2.0 * sigma - rho_old)
            search = (rho_new * rho_old) * search + (2.0 * rho_new / delta) * resid
            rho_old = rho_new
            z = z + search
        return z

    for it in range(ITERS):
        last = it + 1 == ITERS
        if it == 0:
            start = v_coef[0] - v_tdual[0]
            resid = -gram_mul(start)
            for m in range(NC):
                resid += mul(at_hi[m], at_lo[m], (v_tshare[m] + v_sdual[m]).reshape(half, K))
            z = start + chebyshev(resid)
            pl.semaphore_wait(barrier, len(partners))
        zc[it] = z.reshape(NX, NL, B, K)

        to_x = [
            remote(zc.at[it, (x + p) % NX], x_in.at[it, p - 1], samp_dev((x + p) % NX, l))
            for p in x_order
        ]

        z_hi, z_lo = split(z)

        def forward(m):
            ps[it, m] = mul2(a_hi[m], a_lo[m], z_hi, z_lo).reshape(NY, NH, B, K)

        forward(other)
        to_pair = {
            p: remote(
                ps.at[it, other, (y + p) % NY], pair_in.at[it, (y + p) % NY], feat_dev(h, y, other)
            )
            for p in y_order + [0]
        }
        forward(c)
        if it == 0:
            st = [
                remote(v_st.at[:, h], v_st.at[:, h], feat_dev((h + p) % NH, y, c)) for p in h_order
            ]

        to_y = {}
        for g, part in enumerate(groups):
            for p in y_order:
                if g == 0:
                    to_pair[p].wait_recv()
                q = (y + p) % NY
                y_out[it, p, part] = ps[it, c, q, part] + pair_in[it, q, part]
                to_y[g, p] = remote(
                    y_out.at[it, p, part], y_in.at[it, p - 1, part], feat_dev(h, q, c)
                )
        to_pair[0].wait_recv()
        own = ps[it, c, y] + pair_in[it, y]

        summed = zc[it, x]
        for p, copy in zip(x_order, to_x, strict=True):
            copy.wait_recv()
            summed = summed + x_in[it, p - 1]
        l_all[it, l] = summed
        to_l = [
            remote(l_all.at[it, l], l_all.at[it, l], samp_dev(x, (l + p) % NL)) for p in l_order
        ]

        to_h = {}
        for g, part in enumerate(groups):
            total = own[part]
            for p in reversed(y_order):
                to_y[g, p].wait_recv()
                total = total + y_in[it, p - 1, part]
            h_all[it, g, h] = total
            to_h[g] = [
                remote(h_all.at[it, g, h], h_all.at[it, g, h], feat_dev((h + p) % NH, y, c))
                for p in h_order
            ]

        value = v_coef[it] - v_cdual[it]
        half_c[it] = (value - jnp.clip(value, -l1_weight, l1_weight)).reshape(NX, NL, B, K)
        for copy in to_l:
            copy.wait_recv()
        summed = l_all[it, 0]
        for k in range(1, NL):
            summed = summed + l_all[it, k]
        cnew[it, x] = (half_c[it, x] + summed) * (1.0 / (NX * NL + 1))
        from_x = [
            remote(cnew.at[it, x], cnew.at[it, x], samp_dev((x + p) % NX, l)) for p in x_order
        ]

        if it == 0:
            eye = (
                lax.broadcasted_iota(jnp.int32, (feats, feats), 0)
                == lax.broadcasted_iota(jnp.int32, (feats, feats), 1)
            ).astype(f32)
            hi, lo = split(chebyshev(eye))
            q_hi[...] = hi
            q_lo[...] = lo
            for m in range(NC):
                w = mul2(hi, lo, at_hi[m], at_lo[m])
                hi_w, lo_w = split(w)
                w_hi[m] = hi_w
                w_lo[m] = lo_w
        if not last:
            base = jnp.zeros((feats, K), f32)
            for m in range(NC):
                base += mul(w_hi[m], w_lo[m], (ps[it, m] + v_sdual[m]).reshape(half, K))

        if it == 0:
            for copy in st:
                copy.wait()
            sent[:] = [copy for copy in sent if not any(copy is k for k in st)]
        from_y, from_pair = {}, []
        for g, part in enumerate(groups):
            old, goal = v_st[0, part], v_st[1, part]
            resid_t = old - v_sdual[c, y, part] - goal
            half_share = goal + resid_t - jnp.clip(resid_t * 0.5, -huber_width, huber_width)
            for copy in to_h[g]:
                copy.wait_recv()
            total = h_all[it, g, 0]
            for k in range(1, NH):
                total = total + h_all[it, g, k]
            excess = (half_share - total) * (1.0 / (NH * NY * NC + 1))
            exc[it, c, y, part] = excess
            here = exc.at[it, c, y, part]
            for p in y_order:
                from_y[g, p] = remote(here, here, feat_dev(h, (y + p) % NY, c))
            from_pair.append(remote(here, here, feat_dev(h, y, other)))
            share_new = half_share - excess
            if last:
                v_st[1, part] = share_new
            else:
                v_st[2, part] = share_new

        for copy in from_x:
            copy.wait_recv()
        coef_new = cnew[it].reshape(feats, K)
        cdual_new = v_cdual[it] + half_c[it].reshape(feats, K) - coef_new
        tdual_new = v_tdual[it] + zc[it].reshape(feats, K) - coef_new
        if last:
            o_coef[...] = coef_new
            o_cdual[...] = cdual_new
            o_tdual[...] = tdual_new
            o_share[...] = v_st[1, h]
        else:
            v_coef[it + 1] = coef_new
            v_cdual[it + 1] = cdual_new
            v_tdual[it + 1] = tdual_new
            start = coef_new - tdual_new
            base = base + start - mul(q_hi[...], q_lo[...], gram_mul(start))

        for g, part in enumerate(groups):
            for p in reversed(y_order):
                from_y[g, p].wait_recv()
                q = (y - p + NY) % NY
                there = exc.at[it, c, q, part]
                from_pair.append(remote(there, there, feat_dev(h, y, other)))
        z = None if last else base

        for m in (c, other):
            if m is other:
                for copy in from_pair:
                    copy.wait_recv()
            got = exc[it, m]
            if last:
                o_sdual[m] = v_sdual[m] + got
                o_tshare[m] = ps[it, m] + got
            else:
                z = z + mul(w_hi[m], w_lo[m], (got + got).reshape(half, K))
        if not last:
            v_sdual[...] = v_sdual[...] + exc[it]
            v_st[0] = v_st[2]

    for copy in sent:
        copy.wait_send()


def hand_over(*refs):
    n = (len(refs) - 1) // 2
    sem = refs[-1]
    copies = []

    def start(src, dst):
        copies.append(pltpu.make_async_copy(src, dst, sem.at[len(copies)]))
        copies[-1].start()

    for src, dst in zip(refs[:n], refs[n:-1], strict=True):
        if len(src.shape) == 2:
            start(src, dst)
        else:
            for m in range(NC):
                for k in range(NH):
                    start(src.at[m, :, k], dst.at[k, :, m])
    for copy in copies:
        copy.wait()


def shards(data, targets, coef, cdual, tdual, share, sdual, tshare):
    feats = NX * NL * B
    whole = (NH, NY, NC, B)
    perm = (NC, NY, NH, B)
    half = NY * NH * B
    rows = NC * half
    hbm = pl.BlockSpec(memory_space=pltpu.HBM)
    vmem = pl.BlockSpec(memory_space=pltpu.VMEM)
    vm = pltpu.VMEM
    a_sweep = 2 * NG * (NY - 1) + NG * (NH - 1) + 2 * (NX - 1) + (NL - 1) + NY + NG * NY
    copies = ITERS * a_sweep + NH - 1
    shapes = [(feats, K)] * 3 + [(B, K)]
    outs = pl.pallas_call(
        body,
        out_shape=[jax.ShapeDtypeStruct(k, f32) for k in shapes + [perm + (K,)] * 2],
        in_specs=[hbm] * 8,
        out_specs=[vmem] * 6,
        scratch_shapes=[
            vm(perm + (feats,), f32),
            vm((NC, half, feats), bf16),
            vm((NC, half, feats), bf16),
            vm((NC, feats, half), bf16),
            vm((NC, feats, half), bf16),
            vm((NC, feats, half), bf16),
            vm((NC, feats, half), bf16),
            vm((feats, feats), bf16),
            vm((feats, feats), bf16),
            vm((feats, feats), bf16),
            vm((feats, feats), bf16),
            vm((3, NH, B, K), f32),
            vm((ITERS, feats, K), f32),
            vm((ITERS, feats, K), f32),
            vm((ITERS, feats, K), f32),
            vm(perm + (K,), f32),
            vm(perm + (K,), f32),
            vm((ITERS,) + perm + (K,), f32),
            vm((ITERS, NY, NH, B, K), f32),
            vm((ITERS, NY, NH, B, K), f32),
            vm((ITERS, NY - 1, NH, B, K), f32),
            vm((ITERS, NG, NH, NH // NG, B, K), f32),
            vm((ITERS,) + perm + (K,), f32),
            vm((ITERS, NX, NL, B, K), f32),
            vm((ITERS, NX, NL, B, K), f32),
            vm((ITERS, NX - 1, NL, B, K), f32),
            vm((ITERS, NL, NL, B, K), f32),
            vm((ITERS, NX, NL, B, K), f32),
            pltpu.SemaphoreType.DMA((3 * NC * NH + 5,)),
            pltpu.SemaphoreType.DMA((copies,)),
            pltpu.SemaphoreType.DMA((copies,)),
        ],
        compiler_params=pltpu.CompilerParams(
            collective_id=0, has_side_effects=True, vmem_limit_bytes=VMEM_MIB * 1024 * 1024
        ),
    )(
        data.reshape(whole + (feats,)), targets, coef, cdual, tdual[0], share,
        sdual.reshape(whole + (K,)), tshare.reshape(whole + (K,)),
    )
    coef, cdual, tdual, share, sdual, tshare = pl.pallas_call(
        hand_over,
        out_shape=[jax.ShapeDtypeStruct(k, f32) for k in shapes + [whole + (K,)] * 2],
        in_specs=[vmem] * 6,
        out_specs=[hbm] * 6,
        scratch_shapes=[pltpu.SemaphoreType.DMA((4 + 2 * NC * NH,))],
    )(*outs)
    return (coef, cdual, tdual[None], share, sdual.reshape(rows, K), tshare.reshape(1, rows, K))


def solution(mesh):
    return jax.shard_map(
        shards,
        mesh=mesh,
        in_specs=(
            P("samp", "feat"),
            P(("samp", "feat"), None),
            P("feat", None),
            P("feat", None),
            P("samp", "feat", None),
            P(("samp", "feat"), None),
            P("samp", None),
            P("feat", "samp", None),
        ),
        out_specs=(
            P("feat", None),
            P("feat", None),
            P("samp", "feat", None),
            P(("samp", "feat"), None),
            P("samp", None),
            P("feat", "samp", None),
        ),
        check_vma=False,
    )
```

```python
import functools

import jax
import jax.numpy as jnp
from jax import lax
from jax.experimental import pallas as pl
from jax.experimental.pallas import tpu as pltpu
from jax.sharding import PartitionSpec as P

ITERS = 2
CHEB = 5

cheb_low = 1.0
cheb_high = 3.2
l1_weight = 0.2
huber_width = 4.0

NX, NL, NH, NY, NC = 4, 4, 4, 8, 2
B = 16
K = 128
NG = 2
VMEM_MIB = 60

MESH = pl.DeviceIdType.MESH
f32 = jnp.float32
bf16 = jnp.bfloat16


def split(v):
    hi = v.astype(bf16)
    return hi, (v - hi.astype(f32)).astype(bf16)


def mul2(lhs_hi, lhs_lo, hi, lo):
    n = hi.shape[1]
    both = jnp.dot(lhs_hi, jnp.concatenate([hi, lo], axis=1), preferred_element_type=f32)
    return both[:, :n] + both[:, n:] + jnp.dot(lhs_lo, hi, preferred_element_type=f32)


def mul(lhs_hi, lhs_lo, v):
    return mul2(lhs_hi, lhs_lo, *split(v))


def far_first(n):
    return sorted(range(1, n), key=lambda p: -min(p, n - p))


def body(
    data, targets, coef, cdual, tdual, share, sdual, tshare,
    o_coef, o_cdual, o_tdual, o_share, o_sdual, o_tshare,
    a32, a_hi, a_lo, at_hi, at_lo, w_hi, w_lo, gram_hi, gram_lo, q_hi, q_lo,
    v_st, v_coef, v_cdual, v_tdual, v_sdual, v_tshare,
    ps, pair_in, y_out, y_in, h_all, exc, zc, half_c, x_in, l_all, cnew,
    load_sem, send_sem, recv_sem,
):
    half = NY * NH * B
    rows = NC * half
    feats = NX * NL * B
    s, f = lax.axis_index("samp"), lax.axis_index("feat")
    x, l = s // NL, s % NL
    h, y, c = f // (NY * NC), (f // NC) % NY, f % NC
    other = 1 - c

    def feat_dev(h_, y_, c_):
        return (s, (h_ * NY + y_) * NC + c_)

    def samp_dev(x_, l_):
        return (x_ * NL + l_, f)

    y_order, h_order, x_order, l_order = far_first(NY), far_first(NH), far_first(NX), far_first(NL)
    groups = [slice(g * (NH // NG), (g + 1) * (NH // NG)) for g in range(NG)]

    barrier = pltpu.get_barrier_semaphore()
    partners = (
        [feat_dev((h + p) % NH, y, c) for p in h_order]
        + [feat_dev(h, (y + p) % NY, c) for p in y_order]
        + [samp_dev((x + p) % NX, l) for p in x_order]
        + [samp_dev(x, (l + p) % NL) for p in l_order]
        + [feat_dev(h, y, other)]
    )
    for who in partners:
        pl.semaphore_signal(barrier, inc=1, device_id=who, device_id_type=MESH)

    loads = []

    def load(src, dst):
        copy = pltpu.make_async_copy(src, dst, load_sem.at[len(loads)])
        copy.start()
        loads.append(copy)
        return copy

    data_loads = [load(data.at[k, :, m], a32.at[m, :, k]) for m in range(NC) for k in range(NH)]
    out_loads = [
        load(src.at[k, :, m], dst.at[m, :, k])
        for src, dst in ((tshare, v_tshare), (sdual, v_sdual))
        for m in range(NC)
        for k in range(NH)
    ]
    small_loads = [
        load(coef, v_coef.at[0]),
        load(tdual, v_tdual.at[0]),
        load(cdual, v_cdual.at[0]),
        load(share, v_st.at[0, h]),
        load(targets, v_st.at[1, h]),
    ]

    for copy in data_loads:
        copy.wait()
    gram = jnp.zeros((feats, feats), f32)
    for m in range(NC):
        a = a32[m].reshape(half, feats)
        hi, lo = split(a)
        a_hi[m] = hi
        a_lo[m] = lo
        t_hi, t_lo = split(a.T)
        at_hi[m] = t_hi
        at_lo[m] = t_lo
        gram += mul2(t_hi, t_lo, hi, lo)
    hi, lo = split(gram)
    gram_hi[...] = hi
    gram_lo[...] = lo

    for copy in out_loads + small_loads:
        copy.wait()

    def gram_mul(v):
        return mul(gram_hi[...], gram_lo[...], v)

    sent = []
    count = [0]

    def remote(src, dst, who):
        k = count[0]
        count[0] += 1
        copy = pltpu.make_async_remote_copy(
            src_ref=src, dst_ref=dst, send_sem=send_sem.at[k], recv_sem=recv_sem.at[k],
            device_id=who, device_id_type=MESH,
        )
        copy.start()
        sent.append(copy)
        return copy

    theta = (cheb_high + cheb_low) / 2.0
    delta = (cheb_high - cheb_low) / 2.0
    sigma = theta / delta

    def chebyshev(resid):
        search = resid * (1.0 / theta)
        z = search
        rho_old = 1.0 / sigma
        for step in range(CHEB - 1):
            resid = resid - search - gram_mul(search)
            rho_new = 1.0 / (2.0 * sigma - rho_old)
            search = (rho_new * rho_old) * search + (2.0 * rho_new / delta) * resid
            rho_old = rho_new
            z = z + search
        return z

    for it in range(ITERS):
        last = it + 1 == ITERS
        if it == 0:
            start = v_coef[0] - v_tdual[0]
            resid = -gram_mul(start)
            for m in range(NC):
                resid += mul(at_hi[m], at_lo[m], (v_tshare[m] + v_sdual[m]).reshape(half, K))
            z = start + chebyshev(resid)
            pl.semaphore_wait(barrier, len(partners))
        zc[it] = z.reshape(NX, NL, B, K)

        to_x = [
            remote(zc.at[it, (x + p) % NX], x_in.at[it, p - 1], samp_dev((x + p) % NX, l))
            for p in x_order
        ]

        z_hi, z_lo = split(z)

        def forward(m):
            ps[it, m] = mul2(a_hi[m], a_lo[m], z_hi, z_lo).reshape(NY, NH, B, K)

        forward(other)
        to_pair = {
            p: remote(
                ps.at[it, other, (y + p) % NY], pair_in.at[it, (y + p) % NY], feat_dev(h, y, other)
            )
            for p in y_order + [0]
        }
        forward(c)
        if it == 0:
            st = [
                remote(v_st.at[:, h], v_st.at[:, h], feat_dev((h + p) % NH, y, c)) for p in h_order
            ]

        to_y = {}
        for g, part in enumerate(groups):
            for p in y_order:
                if g == 0:
                    to_pair[p].wait_recv()
                q = (y + p) % NY
                y_out[it, p, part] = ps[it, c, q, part] + pair_in[it, q, part]
                to_y[g, p] = remote(
                    y_out.at[it, p, part], y_in.at[it, p - 1, part], feat_dev(h, q, c)
                )
        to_pair[0].wait_recv()
        own = ps[it, c, y] + pair_in[it, y]

        summed = zc[it, x]
        for p, copy in zip(x_order, to_x, strict=True):
            copy.wait_recv()
            summed = summed + x_in[it, p - 1]
        l_all[it, l] = summed
        to_l = [
            remote(l_all.at[it, l], l_all.at[it, l], samp_dev(x, (l + p) % NL)) for p in l_order
        ]

        to_h = {}
        for g, part in enumerate(groups):
            total = own[part]
            for p in reversed(y_order):
                to_y[g, p].wait_recv()
                total = total + y_in[it, p - 1, part]
            h_all[it, g, h] = total
            to_h[g] = [
                remote(h_all.at[it, g, h], h_all.at[it, g, h], feat_dev((h + p) % NH, y, c))
                for p in h_order
            ]

        value = v_coef[it] - v_cdual[it]
        half_c[it] = (value - jnp.clip(value, -l1_weight, l1_weight)).reshape(NX, NL, B, K)
        for copy in to_l:
            copy.wait_recv()
        summed = l_all[it, 0]
        for k in range(1, NL):
            summed = summed + l_all[it, k]
        cnew[it, x] = (half_c[it, x] + summed) * (1.0 / (NX * NL + 1))
        from_x = [
            remote(cnew.at[it, x], cnew.at[it, x], samp_dev((x + p) % NX, l)) for p in x_order
        ]

        if it == 0:
            eye = (
                lax.broadcasted_iota(jnp.int32, (feats, feats), 0)
                == lax.broadcasted_iota(jnp.int32, (feats, feats), 1)
            ).astype(f32)
            hi, lo = split(chebyshev(eye))
            q_hi[...] = hi
            q_lo[...] = lo
            for m in range(NC):
                w = mul2(hi, lo, at_hi[m], at_lo[m])
                hi_w, lo_w = split(w)
                w_hi[m] = hi_w
                w_lo[m] = lo_w
        if not last:
            base = jnp.zeros((feats, K), f32)
            for m in range(NC):
                base += mul(w_hi[m], w_lo[m], (ps[it, m] + v_sdual[m]).reshape(half, K))

        if it == 0:
            for copy in st:
                copy.wait()
            sent[:] = [copy for copy in sent if not any(copy is k for k in st)]
        from_y, from_pair = {}, []
        for g, part in enumerate(groups):
            old, goal = v_st[0, part], v_st[1, part]
            resid_t = old - v_sdual[c, y, part] - goal
            half_share = goal + resid_t - jnp.clip(resid_t * 0.5, -huber_width, huber_width)
            for copy in to_h[g]:
                copy.wait_recv()
            total = h_all[it, g, 0]
            for k in range(1, NH):
                total = total + h_all[it, g, k]
            excess = (half_share - total) * (1.0 / (NH * NY * NC + 1))
            exc[it, c, y, part] = excess
            here = exc.at[it, c, y, part]
            for p in y_order:
                from_y[g, p] = remote(here, here, feat_dev(h, (y + p) % NY, c))
            from_pair.append(remote(here, here, feat_dev(h, y, other)))
            share_new = half_share - excess
            if last:
                v_st[1, part] = share_new
            else:
                v_st[2, part] = share_new

        for copy in from_x:
            copy.wait_recv()
        coef_new = cnew[it].reshape(feats, K)
        cdual_new = v_cdual[it] + half_c[it].reshape(feats, K) - coef_new
        tdual_new = v_tdual[it] + zc[it].reshape(feats, K) - coef_new
        if last:
            o_coef[...] = coef_new
            o_cdual[...] = cdual_new
            o_tdual[...] = tdual_new
            o_share[...] = v_st[1, h]
        else:
            v_coef[it + 1] = coef_new
            v_cdual[it + 1] = cdual_new
            v_tdual[it + 1] = tdual_new
            start = coef_new - tdual_new
            base = base + start - mul(q_hi[...], q_lo[...], gram_mul(start))

        for g, part in enumerate(groups):
            for p in reversed(y_order):
                from_y[g, p].wait_recv()
                q = (y - p + NY) % NY
                there = exc.at[it, c, q, part]
                from_pair.append(remote(there, there, feat_dev(h, y, other)))
        z = None if last else base

        for m in (c, other):
            if m is other:
                for copy in from_pair:
                    copy.wait_recv()
            got = exc[it, m]
            if last:
                o_sdual[m] = v_sdual[m] + got
                o_tshare[m] = ps[it, m] + got
            else:
                z = z + mul(w_hi[m], w_lo[m], (got + got).reshape(half, K))
        if not last:
            v_sdual[...] = v_sdual[...] + exc[it]
            v_st[0] = v_st[2]

    for copy in sent:
        copy.wait_send()


def hand_over(*refs):
    n = (len(refs) - 1) // 2
    sem = refs[-1]
    copies = []

    def start(src, dst):
        copies.append(pltpu.make_async_copy(src, dst, sem.at[len(copies)]))
        copies[-1].start()

    for src, dst in zip(refs[:n], refs[n:-1], strict=True):
        if len(src.shape) == 2:
            start(src, dst)
        else:
            for m in range(NC):
                for k in range(NH):
                    start(src.at[m, :, k], dst.at[k, :, m])
    for copy in copies:
        copy.wait()


def shards(data, targets, coef, cdual, tdual, share, sdual, tshare):
    feats = NX * NL * B
    whole = (NH, NY, NC, B)
    perm = (NC, NY, NH, B)
    half = NY * NH * B
    rows = NC * half
    hbm = pl.BlockSpec(memory_space=pltpu.HBM)
    vmem = pl.BlockSpec(memory_space=pltpu.VMEM)
    vm = pltpu.VMEM
    a_sweep = 2 * NG * (NY - 1) + NG * (NH - 1) + 2 * (NX - 1) + (NL - 1) + NY + NG * NY
    copies = ITERS * a_sweep + NH - 1
    shapes = [(feats, K)] * 3 + [(B, K)]
    outs = pl.pallas_call(
        body,
        out_shape=[pltpu.VMEM(k, f32) for k in shapes + [perm + (K,)] * 2],
        in_specs=[hbm] * 8,
        out_specs=[vmem] * 6,
        scratch_shapes=[
            vm(perm + (feats,), f32),
            vm((NC, half, feats), bf16),
            vm((NC, half, feats), bf16),
            vm((NC, feats, half), bf16),
            vm((NC, feats, half), bf16),
            vm((NC, feats, half), bf16),
            vm((NC, feats, half), bf16),
            vm((feats, feats), bf16),
            vm((feats, feats), bf16),
            vm((feats, feats), bf16),
            vm((feats, feats), bf16),
            vm((3, NH, B, K), f32),
            vm((ITERS, feats, K), f32),
            vm((ITERS, feats, K), f32),
            vm((ITERS, feats, K), f32),
            vm(perm + (K,), f32),
            vm(perm + (K,), f32),
            vm((ITERS,) + perm + (K,), f32),
            vm((ITERS, NY, NH, B, K), f32),
            vm((ITERS, NY, NH, B, K), f32),
            vm((ITERS, NY - 1, NH, B, K), f32),
            vm((ITERS, NG, NH, NH // NG, B, K), f32),
            vm((ITERS,) + perm + (K,), f32),
            vm((ITERS, NX, NL, B, K), f32),
            vm((ITERS, NX, NL, B, K), f32),
            vm((ITERS, NX - 1, NL, B, K), f32),
            vm((ITERS, NL, NL, B, K), f32),
            vm((ITERS, NX, NL, B, K), f32),
            pltpu.SemaphoreType.DMA((3 * NC * NH + 5,)),
            pltpu.SemaphoreType.DMA((copies,)),
            pltpu.SemaphoreType.DMA((copies,)),
        ],
        compiler_params=pltpu.CompilerParams(
            collective_id=0, has_side_effects=True, vmem_limit_bytes=VMEM_MIB * 1024 * 1024
        ),
    )(
        data.reshape(whole + (feats,)), targets, coef, cdual, tdual[0], share,
        sdual.reshape(whole + (K,)), tshare.reshape(whole + (K,)),
    )
    coef, cdual, tdual, share, sdual, tshare = pl.pallas_call(
        hand_over,
        out_shape=[jax.ShapeDtypeStruct(k, f32) for k in shapes + [whole + (K,)] * 2],
        in_specs=[vmem] * 6,
        out_specs=[hbm] * 6,
        scratch_shapes=[pltpu.SemaphoreType.DMA((4 + 2 * NC * NH,))],
        compiler_params=pltpu.CompilerParams(vmem_limit_bytes=4 * 1024 * 1024),
    )(*outs)
    return (coef, cdual, tdual[None], share, sdual.reshape(rows, K), tshare.reshape(1, rows, K))


def solution(mesh):
    return jax.shard_map(
        shards,
        mesh=mesh,
        in_specs=(
            P("samp", "feat"),
            P(("samp", "feat"), None),
            P("feat", None),
            P("feat", None),
            P("samp", "feat", None),
            P(("samp", "feat"), None),
            P("samp", None),
            P("feat", "samp", None),
        ),
        out_specs=(
            P("feat", None),
            P("feat", None),
            P("samp", "feat", None),
            P(("samp", "feat"), None),
            P("samp", None),
            P("feat", "samp", None),
        ),
        check_vma=False,
    )
```

```python
import functools

import jax
import jax.numpy as jnp
from jax import lax
from jax.experimental import pallas as pl
from jax.experimental.pallas import tpu as pltpu
from jax.sharding import PartitionSpec as P

ITERS = 2
CHEB = 5

cheb_low = 1.0
cheb_high = 3.2
l1_weight = 0.2
huber_width = 4.0

NX, NL, NH, NY, NC = 4, 4, 4, 8, 2
B = 16
K = 128
NG = 2
VMEM_MIB = 60

MESH = pl.DeviceIdType.MESH
f32 = jnp.float32
bf16 = jnp.bfloat16


def split(v):
    hi = v.astype(bf16)
    return hi, (v - hi.astype(f32)).astype(bf16)


def mul2(lhs_hi, lhs_lo, hi, lo):
    n = hi.shape[1]
    both = jnp.dot(lhs_hi, jnp.concatenate([hi, lo], axis=1), preferred_element_type=f32)
    return both[:, :n] + both[:, n:] + jnp.dot(lhs_lo, hi, preferred_element_type=f32)


def mul(lhs_hi, lhs_lo, v):
    return mul2(lhs_hi, lhs_lo, *split(v))


def step_polynomial():
    theta = (cheb_high + cheb_low) / 2.0
    delta = (cheb_high - cheb_low) / 2.0
    sigma = theta / delta
    resid = [1.0] + [0.0] * (CHEB - 1)
    search = [k / theta for k in resid]
    z = list(search)
    rho_old = 1.0 / sigma
    for _ in range(CHEB - 1):
        moved = [0.0] + search[:-1]
        resid = [r - d - m for r, d, m in zip(resid, search, moved, strict=True)]
        rho_new = 1.0 / (2.0 * sigma - rho_old)
        search = [
            rho_new * rho_old * d + (2.0 * rho_new / delta) * r
            for d, r in zip(search, resid, strict=True)
        ]
        rho_old = rho_new
        z = [k + d for k, d in zip(z, search, strict=True)]
    return z


def far_first(n):
    return sorted(range(1, n), key=lambda p: -min(p, n - p))


def body(
    data, targets, coef, cdual, tdual, share, sdual, tshare,
    o_coef, o_cdual, o_tdual, o_share, o_sdual, o_tshare,
    a32, a_hi, a_lo, at_hi, at_lo, w_hi, w_lo, gram_hi, gram_lo, powers, q_hi, q_lo,
    v_st, v_coef, v_cdual, v_tdual, v_sdual, v_tshare,
    ps, pair_in, y_out, y_in, h_all, exc, zc, half_c, x_in, l_all, cnew,
    load_sem, send_sem, recv_sem,
):
    half = NY * NH * B
    rows = NC * half
    feats = NX * NL * B
    s, f = lax.axis_index("samp"), lax.axis_index("feat")
    x, l = s // NL, s % NL
    h, y, c = f // (NY * NC), (f // NC) % NY, f % NC
    other = 1 - c

    def feat_dev(h_, y_, c_):
        return (s, (h_ * NY + y_) * NC + c_)

    def samp_dev(x_, l_):
        return (x_ * NL + l_, f)

    y_order, h_order, x_order, l_order = far_first(NY), far_first(NH), far_first(NX), far_first(NL)
    groups = [slice(g * (NH // NG), (g + 1) * (NH // NG)) for g in range(NG)]

    barrier = pltpu.get_barrier_semaphore()
    partners = (
        [feat_dev((h + p) % NH, y, c) for p in h_order]
        + [feat_dev(h, (y + p) % NY, c) for p in y_order]
        + [samp_dev((x + p) % NX, l) for p in x_order]
        + [samp_dev(x, (l + p) % NL) for p in l_order]
        + [feat_dev(h, y, other)]
    )
    for who in partners:
        pl.semaphore_signal(barrier, inc=1, device_id=who, device_id_type=MESH)

    loads = []

    def load(src, dst):
        copy = pltpu.make_async_copy(src, dst, load_sem.at[len(loads)])
        copy.start()
        loads.append(copy)
        return copy

    data_loads = [load(data.at[k, :, m], a32.at[m, :, k]) for m in range(NC) for k in range(NH)]
    out_loads = [
        load(src.at[k, :, m], dst.at[m, :, k])
        for src, dst in ((tshare, v_tshare), (sdual, v_sdual))
        for m in range(NC)
        for k in range(NH)
    ]
    small_loads = [
        load(coef, v_coef.at[0]),
        load(tdual, v_tdual.at[0]),
        load(cdual, v_cdual.at[0]),
        load(share, v_st.at[0, h]),
        load(targets, v_st.at[1, h]),
    ]

    gram = jnp.zeros((feats, feats), f32)
    for m in range(NC):
        for copy in data_loads[m * NH : (m + 1) * NH]:
            copy.wait()
        a = a32[m].reshape(half, feats)
        hi, lo = split(a)
        a_hi[m] = hi
        a_lo[m] = lo
        t_hi, t_lo = split(a.T)
        at_hi[m] = t_hi
        at_lo[m] = t_lo
        gram += mul2(t_hi, t_lo, hi, lo)
    hi, lo = split(gram)
    gram_hi[:feats] = hi
    gram_lo[:feats] = lo
    square = mul2(hi, lo, hi, lo)
    powers[0] = gram
    powers[1] = square
    hi, lo = split(square)
    gram_hi[feats:] = hi
    gram_lo[feats:] = lo

    for copy in out_loads + small_loads:
        copy.wait()

    def gram_mul(v):
        return mul(gram_hi[:feats], gram_lo[:feats], v)

    sent = []
    count = [0]

    def remote(src, dst, who):
        k = count[0]
        count[0] += 1
        copy = pltpu.make_async_remote_copy(
            src_ref=src, dst_ref=dst, send_sem=send_sem.at[k], recv_sem=recv_sem.at[k],
            device_id=who, device_id_type=MESH,
        )
        copy.start()
        sent.append(copy)
        return copy

    e = step_polynomial()

    def chebyshev(resid):
        both = mul(gram_hi[...], gram_lo[...], resid)
        one, two = both[:feats], both[feats:]
        inner = e[2] * resid + e[3] * one + e[4] * two
        return e[0] * resid + e[1] * one + mul(gram_hi[feats:], gram_lo[feats:], inner)

    for it in range(ITERS):
        last = it + 1 == ITERS
        if it == 0:
            start = v_coef[0] - v_tdual[0]
            resid = -gram_mul(start)
            for m in range(NC):
                resid += mul(at_hi[m], at_lo[m], (v_tshare[m] + v_sdual[m]).reshape(half, K))
            z = start + chebyshev(resid)
            pl.semaphore_wait(barrier, len(partners))
        zc[it] = z.reshape(NX, NL, B, K)

        to_x = [
            remote(zc.at[it, (x + p) % NX], x_in.at[it, p - 1], samp_dev((x + p) % NX, l))
            for p in x_order
        ]

        z_hi, z_lo = split(z)

        def forward(m):
            ps[it, m] = mul2(a_hi[m], a_lo[m], z_hi, z_lo).reshape(NY, NH, B, K)

        forward(other)
        to_pair = {
            p: remote(
                ps.at[it, other, (y + p) % NY], pair_in.at[it, (y + p) % NY], feat_dev(h, y, other)
            )
            for p in y_order + [0]
        }
        forward(c)
        if it == 0:
            st = [
                remote(v_st.at[:, h], v_st.at[:, h], feat_dev((h + p) % NH, y, c)) for p in h_order
            ]

        to_y = {}
        for g, part in enumerate(groups):
            for p in y_order:
                if g == 0:
                    to_pair[p].wait_recv()
                q = (y + p) % NY
                y_out[it, p, part] = ps[it, c, q, part] + pair_in[it, q, part]
                to_y[g, p] = remote(
                    y_out.at[it, p, part], y_in.at[it, p - 1, part], feat_dev(h, q, c)
                )
        to_pair[0].wait_recv()
        own = ps[it, c, y] + pair_in[it, y]

        summed = zc[it, x]
        for p, copy in zip(x_order, to_x, strict=True):
            copy.wait_recv()
            summed = summed + x_in[it, p - 1]
        l_all[it, l] = summed
        to_l = [
            remote(l_all.at[it, l], l_all.at[it, l], samp_dev(x, (l + p) % NL)) for p in l_order
        ]

        to_h = {}
        for g, part in enumerate(groups):
            total = own[part]
            for p in reversed(y_order):
                to_y[g, p].wait_recv()
                total = total + y_in[it, p - 1, part]
            h_all[it, g, h] = total
            to_h[g] = [
                remote(h_all.at[it, g, h], h_all.at[it, g, h], feat_dev((h + p) % NH, y, c))
                for p in h_order
            ]

        value = v_coef[it] - v_cdual[it]
        half_c[it] = (value - jnp.clip(value, -l1_weight, l1_weight)).reshape(NX, NL, B, K)
        for copy in to_l:
            copy.wait_recv()
        summed = l_all[it, 0]
        for k in range(1, NL):
            summed = summed + l_all[it, k]
        cnew[it, x] = (half_c[it, x] + summed) * (1.0 / (NX * NL + 1))
        from_x = [
            remote(cnew.at[it, x], cnew.at[it, x], samp_dev((x + p) % NX, l)) for p in x_order
        ]

        if it == 0:
            eye = (
                lax.broadcasted_iota(jnp.int32, (feats, feats), 0)
                == lax.broadcasted_iota(jnp.int32, (feats, feats), 1)
            ).astype(f32)
            inner = e[2] * eye + e[3] * powers[0] + e[4] * powers[1]
            outer = e[0] * eye + e[1] * powers[0]
            hi, lo = split(outer + mul(gram_hi[feats:], gram_lo[feats:], inner))
            q_hi[...] = hi
            q_lo[...] = lo
            for m in range(NC):
                w = mul2(hi, lo, at_hi[m], at_lo[m])
                hi_w, lo_w = split(w)
                w_hi[m] = hi_w
                w_lo[m] = lo_w
        if not last:
            base = jnp.zeros((feats, K), f32)
            for m in range(NC):
                base += mul(w_hi[m], w_lo[m], (ps[it, m] + v_sdual[m]).reshape(half, K))

        if it == 0:
            for copy in st:
                copy.wait()
            sent[:] = [copy for copy in sent if not any(copy is k for k in st)]
        from_y, from_pair = {}, []
        for g, part in enumerate(groups):
            old, goal = v_st[0, part], v_st[1, part]
            resid_t = old - v_sdual[c, y, part] - goal
            half_share = goal + resid_t - jnp.clip(resid_t * 0.5, -huber_width, huber_width)
            for copy in to_h[g]:
                copy.wait_recv()
            total = h_all[it, g, 0]
            for k in range(1, NH):
                total = total + h_all[it, g, k]
            excess = (half_share - total) * (1.0 / (NH * NY * NC + 1))
            exc[it, c, y, part] = excess
            here = exc.at[it, c, y, part]
            for p in y_order:
                from_y[g, p] = remote(here, here, feat_dev(h, (y + p) % NY, c))
            from_pair.append(remote(here, here, feat_dev(h, y, other)))
            share_new = half_share - excess
            if last:
                v_st[1, part] = share_new
            else:
                v_st[2, part] = share_new

        for copy in from_x:
            copy.wait_recv()
        coef_new = cnew[it].reshape(feats, K)
        cdual_new = v_cdual[it] + half_c[it].reshape(feats, K) - coef_new
        tdual_new = v_tdual[it] + zc[it].reshape(feats, K) - coef_new
        if last:
            o_coef[...] = coef_new
            o_cdual[...] = cdual_new
            o_tdual[...] = tdual_new
            o_share[...] = v_st[1, h]
        else:
            v_coef[it + 1] = coef_new
            v_cdual[it + 1] = cdual_new
            v_tdual[it + 1] = tdual_new
            start = coef_new - tdual_new
            base = base + start - mul(q_hi[...], q_lo[...], gram_mul(start))

        for g, part in enumerate(groups):
            for p in reversed(y_order):
                from_y[g, p].wait_recv()
                q = (y - p + NY) % NY
                there = exc.at[it, c, q, part]
                from_pair.append(remote(there, there, feat_dev(h, y, other)))
        z = None if last else base

        for m in (c, other):
            if m is other:
                for copy in from_pair:
                    copy.wait_recv()
            got = exc[it, m]
            if last:
                o_sdual[m] = v_sdual[m] + got
                o_tshare[m] = ps[it, m] + got
            else:
                z = z + mul(w_hi[m], w_lo[m], (got + got).reshape(half, K))
        if not last:
            v_sdual[...] = v_sdual[...] + exc[it]
            v_st[0] = v_st[2]

    for copy in sent:
        copy.wait_send()


def hand_over(*refs):
    n = (len(refs) - 1) // 2
    sem = refs[-1]
    copies = []

    def start(src, dst):
        copies.append(pltpu.make_async_copy(src, dst, sem.at[len(copies)]))
        copies[-1].start()

    for src, dst in zip(refs[:n], refs[n:-1], strict=True):
        if len(src.shape) == 2:
            start(src, dst)
        else:
            for m in range(NC):
                for k in range(NH):
                    start(src.at[m, :, k], dst.at[k, :, m])
    for copy in copies:
        copy.wait()


def shards(data, targets, coef, cdual, tdual, share, sdual, tshare):
    feats = NX * NL * B
    whole = (NH, NY, NC, B)
    perm = (NC, NY, NH, B)
    half = NY * NH * B
    rows = NC * half
    hbm = pl.BlockSpec(memory_space=pltpu.HBM)
    vmem = pl.BlockSpec(memory_space=pltpu.VMEM)
    vm = pltpu.VMEM
    a_sweep = 2 * NG * (NY - 1) + NG * (NH - 1) + 2 * (NX - 1) + (NL - 1) + NY + NG * NY
    copies = ITERS * a_sweep + NH - 1
    shapes = [(feats, K)] * 3 + [(B, K)]
    outs = pl.pallas_call(
        body,
        out_shape=[pltpu.VMEM(k, f32) for k in shapes + [perm + (K,)] * 2],
        in_specs=[hbm] * 8,
        out_specs=[vmem] * 6,
        scratch_shapes=[
            vm(perm + (feats,), f32),
            vm((NC, half, feats), bf16),
            vm((NC, half, feats), bf16),
            vm((NC, feats, half), bf16),
            vm((NC, feats, half), bf16),
            vm((NC, feats, half), bf16),
            vm((NC, feats, half), bf16),
            vm((2 * feats, feats), bf16),
            vm((2 * feats, feats), bf16),
            vm((2, feats, feats), f32),
            vm((feats, feats), bf16),
            vm((feats, feats), bf16),
            vm((3, NH, B, K), f32),
            vm((ITERS, feats, K), f32),
            vm((ITERS, feats, K), f32),
            vm((ITERS, feats, K), f32),
            vm(perm + (K,), f32),
            vm(perm + (K,), f32),
            vm((ITERS,) + perm + (K,), f32),
            vm((ITERS, NY, NH, B, K), f32),
            vm((ITERS, NY, NH, B, K), f32),
            vm((ITERS, NY - 1, NH, B, K), f32),
            vm((ITERS, NG, NH, NH // NG, B, K), f32),
            vm((ITERS,) + perm + (K,), f32),
            vm((ITERS, NX, NL, B, K), f32),
            vm((ITERS, NX, NL, B, K), f32),
            vm((ITERS, NX - 1, NL, B, K), f32),
            vm((ITERS, NL, NL, B, K), f32),
            vm((ITERS, NX, NL, B, K), f32),
            pltpu.SemaphoreType.DMA((3 * NC * NH + 5,)),
            pltpu.SemaphoreType.DMA((copies,)),
            pltpu.SemaphoreType.DMA((copies,)),
        ],
        compiler_params=pltpu.CompilerParams(
            collective_id=0, has_side_effects=True, vmem_limit_bytes=VMEM_MIB * 1024 * 1024
        ),
    )(
        data.reshape(whole + (feats,)), targets, coef, cdual, tdual[0], share,
        sdual.reshape(whole + (K,)), tshare.reshape(whole + (K,)),
    )
    coef, cdual, tdual, share, sdual, tshare = pl.pallas_call(
        hand_over,
        out_shape=[jax.ShapeDtypeStruct(k, f32) for k in shapes + [whole + (K,)] * 2],
        in_specs=[vmem] * 6,
        out_specs=[hbm] * 6,
        scratch_shapes=[pltpu.SemaphoreType.DMA((4 + 2 * NC * NH,))],
        compiler_params=pltpu.CompilerParams(vmem_limit_bytes=4 * 1024 * 1024),
    )(*outs)
    return (coef, cdual, tdual[None], share, sdual.reshape(rows, K), tshare.reshape(1, rows, K))


def solution(mesh):
    return jax.shard_map(
        shards,
        mesh=mesh,
        in_specs=(
            P("samp", "feat"),
            P(("samp", "feat"), None),
            P("feat", None),
            P("feat", None),
            P("samp", "feat", None),
            P(("samp", "feat"), None),
            P("samp", None),
            P("feat", "samp", None),
        ),
        out_specs=(
            P("feat", None),
            P("feat", None),
            P("samp", "feat", None),
            P(("samp", "feat"), None),
            P("samp", None),
            P("feat", "samp", None),
        ),
        check_vma=False,
    )
```
